32 devices in a mesh: groups: 2 (over y), sub: 8 (over z, x), sector: 2 (over core).
Axes of the slice: x: 2, y: 2, z: 4, core: 2. Of those that a mesh axis runs over, the one named last changes fastest.
Arguments:
- ingest: bfloat16 [128, 128, 512], P(('groups', 'sub')), parts along dimension 0, may hold values from -6 to 6
- replica: bfloat16 [2, 512], replicated, may hold values from -0.1875 to 0.1875
- counts: int32 [16], P(('groups', 'sub')), parts along dimension 0, may hold values from 1 to 7, as said below
- track_list: int32 [128], P(('groups', 'sub')), parts along dimension 0, may hold values from -1 to 6, as said below
- deviation: float32 [64], P(('groups', 'sub')), parts along dimension 0, may hold values from -3 to 3
- offsets: int32 [3, 2, 16, 8], P(None, None, ('groups', 'sub'), 'sector'), parts along dimension 2, may hold values from -64 to 64
- fraction: float32 [3, 2, 16, 8], P(None, None, ('groups', 'sub'), 'sector'), parts along dimension 2, may hold values from 0 to 1
Outputs:
- polar_image: bfloat16 [2, 16, 8, 32768], P(None, ('groups', 'sub'), 'sector'), parts along dimension 1
The draws below stay inside these ranges and needn't reach their ends.
There are 2 independent parts, one for each index of `groups`. The reference program is written for one: setup_inputs(seed, part) draws one part's arguments, and reference() takes and returns one part's arrays. A program takes and returns all parts, laid end to end along the dimension named above; an argument that names none is the same for every part. Nothing has to cross between parts.
Inputs may be any that keep to these rules, and one draw needn't show every extreme that they name: Owner a ingests the pulses numbered starts[a] to starts[a] + counts[a] - 1, with starts[a] = counts[0] + ... + counts[a - 1] between a * 4 and a * 4 + 3; the counts sum to 32; in every draw some owner holds 3 pulses of the next owner's subaperture. `track_list`: on owner a, exactly counts[a] of its 8 slots hold the numbers 0 to counts[a] - 1, each once; the other slots hold -1.
All inputs are finite; a program needn't handle non-finite values.
Results may differ from the reference program's by a relative error of at most 0.014.
Values may be sent and summed in bfloat16 or wider, within the bound.
A program may use at most 64 MiB of HBM per device.

```python
import math
import jax
import jax.numpy as jnp
from jax import lax

SAMPLES = 32768
SUB_PULSES = 4
SECTIONS = 3
FILTER_TAPS = 512
BLOCK_SAMPLES = 256
MAX_SHIFT = 64
OWNERS = 8
PULSES = 32
INGEST_SLOTS = 8
ALL_SLOTS = 64
SAMPLE_BLOCKS = 128
SUB_BEAMS = 8


def excess_table(key):
    first_key = jax.random.fold_in(key, 101)
    excess = jax.random.randint(first_key, (OWNERS + 1,), 0, SUB_PULSES)
    chosen = jax.random.randint(jax.random.fold_in(key, 102), (), 0, OWNERS - 1)
    marker = jnp.arange(OWNERS + 1)
    excess = jnp.where(marker == chosen + 1, SUB_PULSES - 1, excess)
    excess = jnp.where(marker == chosen, 0, excess)
    excess = jnp.where((marker == 0) | (marker == OWNERS), 0, excess)
    return excess.astype(jnp.int32)


def draw_counts(key, part):
    excess = excess_table(key)
    return (SUB_PULSES + excess[1:] - excess[:-1]).astype(jnp.int32)


def draw_track_list(key, part):
    excess = excess_table(key)
    key = jax.random.fold_in(key, 5)
    owner_counts = SUB_PULSES + excess[1:] - excess[:-1]
    scores = jax.random.randint(key, (OWNERS, INGEST_SLOTS), 0, 1 << 20) * INGEST_SLOTS + jnp.arange(INGEST_SLOTS)[None, :]
    ranking = jnp.argsort(jnp.argsort(scores, axis=1), axis=1).astype(jnp.int32)
    listed = jnp.where(ranking < owner_counts[:, None], ranking, -1)
    return listed.reshape(OWNERS * INGEST_SLOTS).astype(jnp.int32)


def place_ends(array, own_key, low, top_value):
    shape = array.shape
    index_at = [jax.random.randint(jax.random.fold_in(own_key, axis), (), 0, shape[axis]) for axis in range(len(shape))]
    array = array.at[tuple(index_at)].set(low)
    longest = shape.index(max(shape))
    index_at[longest] = (index_at[longest] + 1) % shape[longest]
    return array.at[tuple(index_at)].set(top_value)


def steps_of(rng, dims, pieces, low, largest):
    def one(axis_at, blocks):
        heights = jax.random.uniform(jax.random.fold_in(jax.random.fold_in(rng, 6), axis_at), (blocks,), jnp.float32, low / len(pieces), largest / len(pieces))
        return jnp.repeat(jnp.exp(heights), dims[axis_at] // blocks).reshape((-1,) + (1,) * (len(dims) - axis_at - 1))

    level = one(*pieces[0])
    for cut in pieces[1:]:
        level = level * one(*cut)
    return level


def centred(key, extent, width, most, cuts=(), dtype=jnp.bfloat16):
    values = jax.random.normal(key, extent, jnp.float32) * width
    if len(cuts) > 0:
        values = steps_of(key, extent, cuts, -0.22, 0.18) * values
    return jnp.clip(values, min=-most, max=most).astype(dtype)


def setup_inputs(seed: int = 0, part: int = 0) -> dict:
    key_of = jax.random.split(jax.random.key(seed), 8)
    part_splits = jax.random.split(jax.random.fold_in(key_of[7], part), 8)
    ingest = centred(part_splits[0], (ALL_SLOTS, SAMPLE_BLOCKS, 2 * BLOCK_SAMPLES), 1.0, 6.0, ((0, 8),))
    replica = centred(key_of[1], (2, FILTER_TAPS), (2 * FILTER_TAPS) ** -0.5, 0.1875)
    counts = draw_counts(jax.random.fold_in(jax.random.fold_in(key_of[7], part), 71), part)
    track_list = draw_track_list(jax.random.fold_in(jax.random.fold_in(key_of[7], part), 71), part)
    deviation = centred(part_splits[4], (PULSES,), 0.5, 3.0, ((0, 8),), jnp.float32)
    offsets = place_ends(jax.random.randint(part_splits[5], (SECTIONS, 2, OWNERS, SUB_BEAMS), -MAX_SHIFT, MAX_SHIFT + 1), jax.random.fold_in(part_splits[5], 1), -MAX_SHIFT, MAX_SHIFT).astype(jnp.int32)
    fraction = jnp.clip(1.0 * jax.random.uniform(part_splits[6], (SECTIONS, 2, OWNERS, SUB_BEAMS), jnp.float32) ** steps_of(part_splits[6], (SECTIONS, 2, OWNERS, SUB_BEAMS), ((2, 8), (3, 2)), -0.2, 0.2), 0.0, 1.0)
    return {"ingest": ingest, "replica": replica, "counts": counts, "track_list": track_list, "deviation": deviation, "offsets": offsets, "fraction": fraction}


BIN_WAVES = 0.85

def filter_blocks(replica, segment):
    taps_count = replica.shape[1]
    window = segment + taps_count
    response = replica.astype(jnp.float32)
    pattern = jnp.concatenate([response, jnp.zeros((2, segment + 1), jnp.float32)], axis=1)
    skewed = jnp.tile(pattern, (1, segment))[:, :segment * window].reshape(2, segment, window)
    banded = jnp.transpose(skewed, (0, 2, 1))
    upper_rows = jnp.concatenate([banded[0], -banded[1]], axis=1)
    lower_rows = jnp.concatenate([banded[1], banded[0]], axis=1)
    matrices = []
    for block_index in range(window // segment):
        first_row = block_index * segment
        matrices.append(jnp.concatenate([upper_rows[first_row:first_row + segment], lower_rows[first_row:first_row + segment]], axis=0))
    return jnp.stack(matrices)

def compress_rows(pulse_rows, filters):
    filter_count = filters.shape[0]
    blocks_count = pulse_rows.shape[1]
    padded = jnp.pad(pulse_rows.astype(jnp.float32), ((0, 0), (0, filter_count - 1), (0, 0)))
    result = jnp.zeros(pulse_rows.shape, jnp.float32)
    for block_index in range(filter_count):
        result = result + jnp.einsum('rkc,cd->rkd', padded[:, block_index:block_index + blocks_count], filters[block_index].astype(jnp.float32), precision=lax.Precision.HIGHEST)
    return result

def cubic_weights(fractions):
    square = fractions * fractions
    cubed = square * fractions
    return (-0.5 * cubed + square - 0.5 * fractions, 1.5 * cubed - 2.5 * square + 1.0, -1.5 * cubed + 2.0 * square + 0.5 * fractions, 0.5 * cubed - 0.5 * square)

def interpolate(child, shifts, fractions):
    length = child.shape[2]
    margin = MAX_SHIFT + 2
    padded = jnp.pad(child, ((0, 0), (0, 0), (margin, margin)))

    def take_row(row_pair, shift_one):
        return lax.dynamic_slice_in_dim(row_pair, (shift_one + (margin - 1)).astype(jnp.int32), length + 3, 1)
    window = jax.vmap(take_row, in_axes=(1, 0), out_axes=1)(padded, shifts)
    weights = cubic_weights(fractions)
    summed = weights[0][None, :, None] * window[:, :, 0:length].astype(jnp.float32)
    for tap_index in range(1, 4):
        summed = summed + weights[tap_index][None, :, None] * window[:, :, tap_index:tap_index + length].astype(jnp.float32)
    rotation = 2.0 * math.pi * BIN_WAVES * (shifts.astype(jnp.float32) + fractions)
    cosine = jnp.cos(rotation)[:, None]
    sine_part = jnp.sin(rotation)[:, None]
    return jnp.stack([cosine * summed[0] - sine_part * summed[1], sine_part * summed[0] + cosine * summed[1]])

def merge_pair(lower_image, upper_image, shifts, fractions):
    combined = interpolate(lower_image, shifts[0], fractions[0]) + interpolate(upper_image, shifts[1], fractions[1])
    return (combined * (1.0 / math.sqrt(2.0))).astype(jnp.bfloat16)

def reference(ingest, replica, counts, track_list, deviation, offsets, fraction):
    starts = (jnp.cumsum(counts) - counts).astype(jnp.int32)
    slot_owner = (jnp.arange(ALL_SLOTS) // INGEST_SLOTS).astype(jnp.int32)
    destination = (starts[slot_owner] + track_list).astype(jnp.int32)
    destination = jnp.where(track_list >= 0, destination, PULSES).astype(jnp.int32)
    raw_pulses = jnp.zeros((PULSES, SAMPLE_BLOCKS, 2 * BLOCK_SAMPLES), jnp.bfloat16).at[destination].set(ingest, mode='drop')
    filters = filter_blocks(replica, BLOCK_SAMPLES)
    grouped = raw_pulses.reshape(OWNERS, SUB_PULSES, SAMPLE_BLOCKS, 2 * BLOCK_SAMPLES)
    compressed = lax.map(lambda pulse_rows: compress_rows(pulse_rows, filters).astype(jnp.bfloat16), grouped)
    beam_index = jnp.arange(SUB_BEAMS).astype(jnp.float32)
    beam_angle = (beam_index + 0.5) / SUB_BEAMS - 0.5
    pulse_index = jnp.arange(SUB_PULSES).astype(jnp.float32)
    position = 2.0 * (pulse_index - (SUB_PULSES - 1) / 2.0)[None, :] + deviation.reshape(OWNERS, SUB_PULSES)
    phase_angle = 2.0 * math.pi * position[:, None, :] * beam_angle[None, :, None]
    scale = 1.0 / math.sqrt(SUB_PULSES)
    real_weight = (jnp.cos(phase_angle) * scale).astype(jnp.bfloat16)
    imag_weight = (jnp.sin(phase_angle) * scale).astype(jnp.bfloat16)
    stacked = jnp.stack([jnp.stack([real_weight, -imag_weight]), jnp.stack([imag_weight, real_weight])])
    spread = compressed.reshape(OWNERS, SUB_PULSES, SAMPLE_BLOCKS, 2, BLOCK_SAMPLES)
    images = jnp.einsum('oiabp,apkis->aobks', stacked.astype(jnp.float32), spread.astype(jnp.float32), precision=lax.Precision.HIGHEST)
    images = images.astype(jnp.bfloat16).reshape(OWNERS, 2, SUB_BEAMS, SAMPLES)
    owner_index = jnp.arange(OWNERS).astype(jnp.int32)
    for section_index in range(SECTIONS):
        stride = 1 << section_index
        lower_index = (owner_index - owner_index // stride % 2 * stride).astype(jnp.int32)
        upper_index = (lower_index + stride).astype(jnp.int32)
        section_shifts = jnp.transpose(offsets[section_index], (1, 0, 2))
        section_fracs = jnp.transpose(fraction[section_index], (1, 0, 2))
        current = images

        def merge_owner(item):
            return merge_pair(current[item[0]], current[item[1]], item[2], item[3])
        images = lax.map(merge_owner, (lower_index, upper_index, section_shifts, section_fracs))
    return jnp.transpose(images, (1, 0, 2, 3))
```

```python
import functools
import math

import jax
import jax.numpy as jnp
from jax import lax
from jax.experimental import pallas as pl
from jax.experimental.pallas import tpu as pltpu
from jax.sharding import PartitionSpec as P

SECTIONS = 3
HALO = 72
CHUNK = 32
MESH = pl.DeviceIdType.MESH
F32 = jnp.float32
BF16 = jnp.bfloat16


def cos_sin_cycles(cycles):
    angle = (2.0 * math.pi) * (cycles - jnp.floor(cycles + 0.5))
    return jnp.cos(angle), jnp.sin(angle)


def cubic_weights(fractions):
    square = fractions * fractions
    cubed = square * fractions
    return (
        -0.5 * cubed + square - 0.5 * fractions,
        1.5 * cubed - 2.5 * square + 1.0,
        -1.5 * cubed + 2.0 * square + 0.5 * fractions,
        0.5 * cubed - 0.5 * square,
    )


def build_filter(replica_ref, filter_ref, segment):
    taps = replica_ref.shape[1]
    window = segment + taps
    row = lax.broadcasted_iota(jnp.int32, (16, window), 0)
    for part in range(2):
        response = replica_ref[part : part + 1, :].astype(F32)
        line = jnp.concatenate([response, jnp.zeros((1, segment), F32)], axis=1)
        base = jnp.broadcast_to(line, (16, window))
        for bit in range(4):
            base = jnp.where((row >> bit) & 1 == 1, pltpu.roll(base, 1 << bit, 1), base)
        for group in range(segment // 16):
            band = base if group == 0 else pltpu.roll(base, 16 * group, 1)
            band_up = band.astype(BF16)
            band_neg = (-band).astype(BF16)
            rows = slice(16 * group, 16 * group + 16)
            rows_low = slice(segment + 16 * group, segment + 16 * group + 16)
            for j in range(window // segment):
                piece = slice(j * segment, (j + 1) * segment)
                re_at = slice(2 * j * segment, (2 * j + 1) * segment)
                im_at = slice((2 * j + 1) * segment, (2 * j + 2) * segment)
                if part == 0:
                    filter_ref[rows, re_at] = band_up[:, piece]
                    filter_ref[rows_low, im_at] = band_up[:, piece]
                else:
                    filter_ref[rows, im_at] = band_up[:, piece]
                    filter_ref[rows_low, re_at] = band_neg[:, piece]


def kernel(
    owners,
    pulses,
    ingest_ref,
    replica_ref,
    counts_ref,
    track_ref,
    deviation_ref,
    shift_ref,
    offsets_ref,
    fraction_ref,
    out_ref,
    count_mine,
    count_all,
    filter_ref,
    stacked_ref,
    comp_ref,
    excess_ref,
    hand_ref,
    acc_ref,
    image_ref,
    other_ref,
    wide_ref,
    count_send,
    count_recv,
    hand_send,
    hand_recv,
    pair_send,
    pair_recv,
    merge_send,
    merge_recv,
):
    slots, blocks, both = ingest_ref.shape
    segment = both // 2
    moved = pulses - 1
    me = lax.axis_index("sub")
    sector = lax.axis_index("sector")

    def peer(step):
        return lax.rem(me + step, owners)

    barrier = pltpu.get_barrier_semaphore()

    def greet(step, carry):
        pl.semaphore_signal(barrier, inc=1, device_id={"sub": peer(step)}, device_id_type=MESH)
        return carry

    lax.fori_loop(1, owners, greet, 0)
    pl.semaphore_signal(barrier, inc=1, device_id={"sector": 1 - sector}, device_id_type=MESH)
    count_mine[...] = jnp.zeros(count_mine.shape, jnp.int32) + counts_ref[0]
    build_filter(replica_ref, filter_ref, segment)
    pl.semaphore_wait(barrier, owners)

    def count_copy(step, source):
        return pltpu.make_async_remote_copy(
            src_ref=count_mine,
            dst_ref=count_all.at[source],
            send_sem=count_send.at[step],
            recv_sem=count_recv.at[source],
            device_id={"sub": peer(step)},
            device_id_type=MESH,
        )

    def send_count(step, carry):
        count_copy(step, me).start()
        return carry

    lax.fori_loop(1, owners, send_count, 0)

    for slot in range(slots):
        rows = slice(slot * blocks, (slot + 1) * blocks)
        data = ingest_ref[slot]
        stacked_ref[rows, 0:both] = data
        wide = data.astype(F32)
        at = lax.broadcasted_iota(jnp.int32, wide.shape, 0)
        for j in range(1, stacked_ref.shape[1] // both):
            later = jnp.where(at < blocks - j, pltpu.roll(wide, blocks - j, 0), 0.0)
            stacked_ref[rows, j * both : (j + 1) * both] = later.astype(BF16)

    def compress(slot, carry):
        rows = pl.ds(pl.multiple_of(slot * blocks, blocks), blocks)
        comp_ref[slot] = lax.dot_general(
            filter_ref[...],
            stacked_ref[rows, :],
            (((1,), (1,)), ((), ())),
            preferred_element_type=F32,
        ).astype(BF16)
        return carry

    lax.fori_loop(0, slots, compress, 0)

    def wait_count(step, carry):
        count_copy(step, peer(step)).wait_recv()
        return carry

    lax.fori_loop(1, owners, wait_count, 0)
    count_all[me] = count_mine[...]

    def add_count(source, total):
        return total + jnp.where(source < me, count_all[source], 0)

    starts = lax.fori_loop(0, owners, add_count, jnp.zeros((8, 128), jnp.int32))
    track = track_ref[...]
    place = starts[0:1, 0:1] - me * pulses + track

    def chosen(target):
        return jnp.where((place == target) & (track >= 0), 1.0, 0.0).astype(F32)

    picks = [chosen(pulses + q) for q in range(moved)]
    pick_at = [
        [jnp.broadcast_to(picks[q][:, s : s + 1], (16, blocks)) for s in range(slots)]
        for q in range(moved)
    ]
    part_row = sector * segment

    def pick_rows(step, carry):
        at = pl.ds(pl.multiple_of(part_row + step * 16, 16), 16)
        to = pl.ds(pl.multiple_of(step * 16, 16), 16)
        values = [comp_ref[s, at, :].astype(F32) for s in range(slots)]
        for q in range(moved):
            total = pick_at[q][0] * values[0]
            for s in range(1, slots):
                total = total + pick_at[q][s] * values[s]
            excess_ref[q, to, :] = total.astype(BF16)
        return carry

    lax.fori_loop(0, segment // 16, pick_rows, 0)

    def hand_copy(q):
        return pltpu.make_async_remote_copy(
            src_ref=excess_ref.at[q],
            dst_ref=hand_ref.at[q, sector],
            send_sem=hand_send.at[q],
            recv_sem=hand_recv.at[q],
            device_id={"sub": peer(1)},
            device_id_type=MESH,
        )

    def pair_copy(q, part):
        return pltpu.make_async_remote_copy(
            src_ref=hand_ref.at[q, part],
            dst_ref=hand_ref.at[q, part],
            send_sem=pair_send.at[q],
            recv_sem=pair_recv.at[q],
            device_id={"sector": 1 - sector},
            device_id_type=MESH,
        )

    for q in range(moved):
        hand_copy(q).start()

    beams = pulses
    beam_index = lax.broadcasted_iota(jnp.int32, (beams, 1), 0) + sector * beams
    beam_angle = (beam_index.astype(F32) + 0.5) / (2.0 * beams) - 0.5
    pulse_index = lax.broadcasted_iota(jnp.int32, (1, pulses), 1).astype(F32)
    position = 2.0 * (pulse_index - (pulses - 1) / 2.0) + deviation_ref[...]
    cosine, sine = cos_sin_cycles(position * beam_angle)
    scale = 1.0 / math.sqrt(pulses)
    weight_re = (cosine * scale).astype(BF16).astype(F32)
    weight_im = (sine * scale).astype(BF16).astype(F32)
    slot_re = jnp.zeros((beams, slots), F32)
    slot_im = jnp.zeros((beams, slots), F32)
    for p in range(pulses):
        select = chosen(p)
        slot_re = slot_re + weight_re[:, p : p + 1] * select
        slot_im = slot_im + weight_im[:, p : p + 1] * select

    def spread(values, b, s, rows):
        return jnp.broadcast_to(values[b : b + 1, s : s + 1], (rows, blocks))

    for b in range(beams):
        own_re = [spread(slot_re, b, s, 16) for s in range(slots)]
        own_im = [spread(slot_im, b, s, 16) for s in range(slots)]

        def own_rows(step, carry):
            at = pl.ds(pl.multiple_of(step * 16, 16), 16)
            at_im = pl.ds(pl.multiple_of(segment + step * 16, 16), 16)
            total_re = jnp.zeros((16, blocks), F32)
            total_im = jnp.zeros((16, blocks), F32)
            for s in range(slots):
                real = comp_ref[s, at, :].astype(F32)
                imag = comp_ref[s, at_im, :].astype(F32)
                total_re = total_re + (own_re[s] * real - own_im[s] * imag)
                total_im = total_im + (own_im[s] * real + own_re[s] * imag)
            acc_ref[b, 0, at, :] = total_re
            acc_ref[b, 1, at, :] = total_im
            return carry

        lax.fori_loop(0, segment // 16, own_rows, 0)

    def section_terms(s):
        upper = (me >> s) & 1
        found = []
        for c in range(2):
            f = fraction_ref[s, c]
            o = offsets_ref[s, c]
            turn = lax.rem(17 * (o + 100), 20).astype(F32) * 0.05
            cosine, sine = cos_sin_cycles(turn + 0.85 * f)
            found.append(list(cubic_weights(f)) + [cosine * math.sqrt(0.5), sine * math.sqrt(0.5)])
        is_upper = jnp.zeros(fraction_ref.shape[2:], jnp.int32) + upper == 1
        own = [jnp.where(is_upper, u, l) for l, u in zip(*found)]
        far = [jnp.where(is_upper, l, u) for l, u in zip(*found)]
        return own, far

    terms = [section_terms(s) for s in range(SECTIONS)]

    def merge_copy(s, b):
        return pltpu.make_async_remote_copy(
            src_ref=image_ref.at[s, b],
            dst_ref=other_ref.at[s, b],
            send_sem=merge_send.at[s, b],
            recv_sem=merge_recv.at[s, b],
            device_id={"sub": me ^ (1 << s)},
            device_id_type=MESH,
        )

    lane = lax.broadcasted_iota(jnp.int32, (HALO, blocks), 1)

    def widen(source):
        for part in range(2):
            value = source[part].astype(F32)
            wide_ref[part, HALO : HALO + segment, :] = value
            wide_ref[part, 0:HALO, :] = jnp.where(
                lane > 0, pltpu.roll(value[segment - HALO :], 1, 1), 0.0
            )
            wide_ref[part, HALO + segment :, :] = jnp.where(
                lane < blocks - 1, pltpu.roll(value[:HALO], blocks - 1, 1), 0.0
            )

    def interpolate(s, b, far, store):
        upper = (me >> s) & 1
        child = 1 - upper if far else upper
        first = shift_ref[s, child, 0, b] + (HALO - 1)
        w0, w1, w2, w3, cosine, sine = [
            jnp.broadcast_to(t[:, b : b + 1], (CHUNK, blocks)) for t in terms[s][int(far)]
        ]

        def rows(step, carry):
            start = first + step * CHUNK
            sums = []
            for part in range(2):
                taps = [wide_ref[part, pl.ds(start + t, CHUNK), :] for t in range(4)]
                sums.append(w0 * taps[0] + w1 * taps[1] + w2 * taps[2] + w3 * taps[3])
            at = pl.ds(pl.multiple_of(step * CHUNK, CHUNK), CHUNK)
            store(at, 0, cosine * sums[0] - sine * sums[1])
            store(at, 1, sine * sums[0] + cosine * sums[1])
            return carry

        lax.fori_loop(0, segment // CHUNK, rows, 0)

    def own_side(s, b):
        widen(image_ref.at[s, b])

        def store(at, part, value):
            acc_ref[b, part, at, :] = value

        interpolate(s, b, False, store)

    def far_side(s, b):
        merge_copy(s, b).wait_recv()
        widen(other_ref.at[s, b])
        if s + 1 < SECTIONS:

            def store(at, part, value):
                image_ref[s + 1, b, part, at, :] = (acc_ref[b, part, at, :] + value).astype(BF16)

            interpolate(s, b, True, store)
            merge_copy(s + 1, b).start()
            own_side(s + 1, b)
        else:

            def store(at, part, value):
                acc_ref[b, part, at, :] = acc_ref[b, part, at, :] + value

            interpolate(s, b, True, store)
            for part in range(2):
                out_ref[part, b] = jnp.transpose(acc_ref[b, part]).astype(BF16)

    for q in range(moved):
        hand_copy(q).wait_recv()
        pair_copy(q, sector).start()
    for q in range(moved):
        pair_copy(q, 1 - sector).wait_recv()

    for b in range(beams):
        far_re = [spread(weight_re, b, q, 16) for q in range(moved)]
        far_im = [spread(weight_im, b, q, 16) for q in range(moved)]

        def first_rows(step, carry):
            at = pl.ds(pl.multiple_of(step * 16, 16), 16)
            total_re = acc_ref[b, 0, at, :]
            total_im = acc_ref[b, 1, at, :]
            for q in range(moved):
                real = hand_ref[q, 0, at, :].astype(F32)
                imag = hand_ref[q, 1, at, :].astype(F32)
                total_re = total_re + (far_re[q] * real - far_im[q] * imag)
                total_im = total_im + (far_im[q] * real + far_re[q] * imag)
            image_ref[0, b, 0, at, :] = total_re.astype(BF16)
            image_ref[0, b, 1, at, :] = total_im.astype(BF16)
            return carry

        lax.fori_loop(0, segment // 16, first_rows, 0)
        merge_copy(0, b).start()
    for b in range(beams):
        own_side(0, b)
    for wave in range(beams + SECTIONS - 1):
        for s in range(SECTIONS - 1, -1, -1):
            if 0 <= wave - s < beams:
                far_side(s, wave - s)

    def end_count(step, carry):
        count_copy(step, me).wait_send()
        return carry

    lax.fori_loop(1, owners, end_count, 0)
    for q in range(moved):
        hand_copy(q).wait_send()
        pair_copy(q, sector).wait_send()
    for s in range(SECTIONS):
        for b in range(beams):
            merge_copy(s, b).wait_send()


def on_device(owners, ingest, replica, counts, track_list, deviation, offsets, fraction):
    slots, blocks, both = ingest.shape
    pulses = slots // 2
    segment = both // 2
    taps = replica.shape[1]
    depth = (segment + taps) // segment
    moved = pulses - 1
    vmem = pl.BlockSpec(memory_space=pltpu.VMEM)
    smem = pl.BlockSpec(memory_space=pltpu.SMEM)
    dma = pltpu.SemaphoreType.DMA
    result = pl.pallas_call(
        functools.partial(kernel, owners, pulses),
        out_shape=jax.ShapeDtypeStruct((2, pulses, blocks, segment), BF16),
        in_specs=[vmem, vmem, smem, vmem, vmem, smem, vmem, vmem],
        out_specs=vmem,
        scratch_shapes=[
            pltpu.VMEM((8, 128), jnp.int32),
            pltpu.VMEM((owners, 8, 128), jnp.int32),
            pltpu.VMEM((both, depth * both), BF16),
            pltpu.VMEM((slots * blocks, depth * both), BF16),
            pltpu.VMEM((slots, both, blocks), BF16),
            pltpu.VMEM((moved, segment, blocks), BF16),
            pltpu.VMEM((moved, 2, segment, blocks), BF16),
            pltpu.VMEM((pulses, 2, segment, blocks), F32),
            pltpu.VMEM((SECTIONS, pulses, 2, segment, blocks), BF16),
            pltpu.VMEM((SECTIONS, pulses, 2, segment, blocks), BF16),
            pltpu.VMEM((2, segment + 2 * HALO, blocks), F32),
            dma((owners,)),
            dma((owners,)),
            dma((moved,)),
            dma((moved,)),
            dma((moved,)),
            dma((moved,)),
            dma((SECTIONS, pulses)),
            dma((SECTIONS, pulses)),
        ],
        compiler_params=pltpu.CompilerParams(
            collective_id=0, has_side_effects=True, vmem_limit_bytes=40 * 1024 * 1024
        ),
    )(
        ingest,
        replica,
        counts,
        track_list.reshape(1, slots),
        deviation.reshape(1, pulses),
        offsets,
        offsets,
        fraction,
    )
    return result.reshape(2, 1, pulses, blocks * segment)


def solution(mesh):
    return jax.shard_map(
        functools.partial(on_device, mesh.shape["sub"]),
        mesh=mesh,
        in_specs=(
            P(("groups", "sub"), None, None),
            P(),
            P(("groups", "sub")),
            P(("groups", "sub")),
            P(("groups", "sub")),
            P(None, None, ("groups", "sub"), "sector"),
            P(None, None, ("groups", "sub"), "sector"),
        ),
        out_specs=P(None, ("groups", "sub"), "sector", None),
        check_vma=False,
    )
```

```python
import functools
import math

import jax
import jax.numpy as jnp
from jax import lax
from jax.experimental import pallas as pl
from jax.experimental.pallas import tpu as pltpu
from jax.sharding import PartitionSpec as P

SECTIONS = 3
HALO = 72
CHUNK = 32
MESH = pl.DeviceIdType.MESH
F32 = jnp.float32
BF16 = jnp.bfloat16


def cos_sin_cycles(cycles):
    angle = (2.0 * math.pi) * (cycles - jnp.floor(cycles + 0.5))
    return jnp.cos(angle), jnp.sin(angle)


def cubic_weights(fractions):
    square = fractions * fractions
    cubed = square * fractions
    return (
        -0.5 * cubed + square - 0.5 * fractions,
        1.5 * cubed - 2.5 * square + 1.0,
        -1.5 * cubed + 2.0 * square + 0.5 * fractions,
        0.5 * cubed - 0.5 * square,
    )


def build_filter(replica_ref, filter_ref, segment, parts):
    taps = replica_ref.shape[1]
    window = segment + taps
    row = lax.broadcasted_iota(jnp.int32, (16, window), 0)
    for part in parts:
        response = replica_ref[part : part + 1, :].astype(F32)
        line = jnp.concatenate([response, jnp.zeros((1, segment), F32)], axis=1)
        base = jnp.broadcast_to(line, (16, window))
        for bit in range(4):
            base = jnp.where((row >> bit) & 1 == 1, pltpu.roll(base, 1 << bit, 1), base)
        for group in range(segment // 16):
            band = base if group == 0 else pltpu.roll(base, 16 * group, 1)
            band_up = band.astype(BF16)
            band_neg = (-band).astype(BF16)
            rows = slice(16 * group, 16 * group + 16)
            rows_low = slice(segment + 16 * group, segment + 16 * group + 16)
            for j in range(window // segment):
                piece = slice(j * segment, (j + 1) * segment)
                re_at = slice(2 * j * segment, (2 * j + 1) * segment)
                im_at = slice((2 * j + 1) * segment, (2 * j + 2) * segment)
                if part == 0:
                    filter_ref[rows, re_at] = band_up[:, piece]
                    filter_ref[rows_low, im_at] = band_up[:, piece]
                else:
                    filter_ref[rows, im_at] = band_up[:, piece]
                    filter_ref[rows_low, re_at] = band_neg[:, piece]


def kernel(
    owners,
    pulses,
    ingest_hbm,
    replica_hbm,
    counts_hbm,
    track_hbm,
    deviation_hbm,
    offsets_hbm,
    fraction_hbm,
    out_ref,
    ingest_ref,
    replica_ref,
    counts_ref,
    track_ref,
    deviation_ref,
    shift_ref,
    offsets_ref,
    fraction_ref,
    load_sem,
    count_mine,
    count_all,
    filter_ref,
    stacked_ref,
    comp_ref,
    excess_ref,
    hand_ref,
    owned_ref,
    acc_ref,
    image_ref,
    other_ref,
    wide_ref,
    count_send,
    count_recv,
    hand_send,
    hand_recv,
    pair_send,
    pair_recv,
    merge_send,
    merge_recv,
):
    slots, blocks, both = ingest_ref.shape
    segment = both // 2
    moved = pulses - 1
    me = lax.axis_index("sub")
    sector = lax.axis_index("sector")

    def peer(step):
        return lax.rem(me + step, owners)

    barrier = pltpu.get_barrier_semaphore()

    def greet(step, carry):
        pl.semaphore_signal(barrier, inc=1, device_id={"sub": peer(step)}, device_id_type=MESH)
        return carry

    lax.fori_loop(1, owners, greet, 0)
    pl.semaphore_signal(barrier, inc=1, device_id={"sector": 1 - sector}, device_id_type=MESH)
    loads = [
        pltpu.make_async_copy(source, target, load_sem.at[i])
        for i, (source, target) in enumerate(
            [
                (replica_hbm, replica_ref),
                (counts_hbm, counts_ref),
                (track_hbm, track_ref),
                (deviation_hbm, deviation_ref),
                (offsets_hbm, shift_ref),
                (offsets_hbm, offsets_ref),
                (fraction_hbm, fraction_ref),
                (ingest_hbm, ingest_ref),
            ]
        )
    ]
    for load in loads:
        load.start()
    loads[0].wait()
    build_filter(replica_ref, filter_ref, segment, [0])
    loads[1].wait()
    count_mine[...] = jnp.zeros(count_mine.shape, jnp.int32) + counts_ref[0]
    pl.semaphore_wait(barrier, owners)

    def count_copy(step, source):
        return pltpu.make_async_remote_copy(
            src_ref=count_mine,
            dst_ref=count_all.at[source],
            send_sem=count_send.at[step],
            recv_sem=count_recv.at[source],
            device_id={"sub": peer(step)},
            device_id_type=MESH,
        )

    def send_count(step, carry):
        count_copy(step, me).start()
        return carry

    lax.fori_loop(1, owners, send_count, 0)

    build_filter(replica_ref, filter_ref, segment, [1])
    for load in loads[2:]:
        load.wait()

    def wait_count(step, carry):
        count_copy(step, peer(step)).wait_recv()
        return carry

    lax.fori_loop(1, owners, wait_count, 0)
    count_all[me] = count_mine[...]

    def add_count(source, total):
        return total + jnp.where(source < me, count_all[source], 0)

    starts = lax.fori_loop(0, owners, add_count, jnp.zeros((8, 128), jnp.int32))
    track = track_ref[...]
    place = starts[0:1, 0:1] - me * pulses + track

    def chosen(target):
        return jnp.where((place == target) & (track >= 0), 1.0, 0.0).astype(F32)

    def pick_at(target):
        pick = chosen(target)
        return [
            jnp.broadcast_to(pick[:, s : s + 1], (16, 128)).astype(BF16) for s in range(slots)
        ]

    def pick_piece(picks, at, lanes):
        values = [ingest_ref[s, at, lanes] for s in range(slots)]
        totals = []
        for pick in picks:
            total = pick[0] * values[0]
            for s in range(1, slots):
                total = total + pick[s] * values[s]
            totals.append(total)
        return totals

    half = blocks // 2
    pieces = [slice(128 * i, 128 * (i + 1)) for i in range(both // 128)]
    excess_picks = [pick_at(pulses + q) for q in range(moved)]

    def pick_rows(step, carry):
        at = pl.ds(pl.multiple_of(sector * half + step * 16, 16), 16)
        to = pl.ds(pl.multiple_of(step * 16, 16), 16)
        for lanes in pieces:
            for q, total in enumerate(pick_piece(excess_picks, at, lanes)):
                excess_ref[q, to, lanes] = total
        return carry

    lax.fori_loop(0, half // 16, pick_rows, 0)

    def half_of(part):
        return pl.ds(pl.multiple_of(part * half, half), half)

    def hand_copy(q):
        return pltpu.make_async_remote_copy(
            src_ref=excess_ref.at[q],
            dst_ref=hand_ref.at[q, half_of(sector)],
            send_sem=hand_send.at[q],
            recv_sem=hand_recv.at[q],
            device_id={"sub": peer(1)},
            device_id_type=MESH,
        )

    def pair_copy(q, part):
        return pltpu.make_async_remote_copy(
            src_ref=hand_ref.at[q, half_of(part)],
            dst_ref=hand_ref.at[q, half_of(part)],
            send_sem=pair_send.at[q],
            recv_sem=pair_recv.at[q],
            device_id={"sector": 1 - sector},
            device_id_type=MESH,
        )

    for q in range(moved):
        hand_copy(q).start()

    own_picks = [pick_at(p) for p in range(pulses)]

    def own_pick_rows(step, carry):
        at = pl.ds(pl.multiple_of(step * 16, 16), 16)
        for lanes in pieces:
            for p, total in enumerate(pick_piece(own_picks, at, lanes)):
                owned_ref[p, at, lanes] = total
        return carry

    lax.fori_loop(0, blocks // 16, own_pick_rows, 0)

    def stack(data, first):
        rows = slice(first * blocks, (first + 1) * blocks)
        stacked_ref[rows, 0:both] = data
        wide = data.astype(F32)
        at = lax.broadcasted_iota(jnp.int32, wide.shape, 0)
        for j in range(1, stacked_ref.shape[1] // both):
            later = jnp.where(at < blocks - j, pltpu.roll(wide, blocks - j, 0), 0.0)
            stacked_ref[rows, j * both : (j + 1) * both] = later.astype(BF16)

    def compress(first, many):
        found = lax.dot_general(
            filter_ref[...],
            stacked_ref[first * blocks : (first + many) * blocks, :],
            (((1,), (1,)), ((), ())),
            preferred_element_type=F32,
        ).astype(BF16)
        for i in range(many):
            comp_ref[first + i] = found[:, i * blocks : (i + 1) * blocks]

    for p in range(pulses):
        stack(owned_ref[p], p)
    for p in range(0, pulses, 2):
        compress(p, 2)

    beams = pulses
    beam_index = lax.broadcasted_iota(jnp.int32, (beams, 1), 0) + sector * beams
    beam_angle = (beam_index.astype(F32) + 0.5) / (2.0 * beams) - 0.5
    pulse_index = lax.broadcasted_iota(jnp.int32, (1, pulses), 1).astype(F32)
    position = 2.0 * (pulse_index - (pulses - 1) / 2.0) + deviation_ref[...]
    cosine, sine = cos_sin_cycles(position * beam_angle)
    scale = 1.0 / math.sqrt(pulses)
    weight_re = (cosine * scale).astype(BF16).astype(F32)
    weight_im = (sine * scale).astype(BF16).astype(F32)
    def spread(values, b, s, rows):
        return jnp.broadcast_to(values[b : b + 1, s : s + 1], (rows, blocks))

    for b in range(beams):
        own_re = [spread(weight_re, b, s, 16) for s in range(pulses)]
        own_im = [spread(weight_im, b, s, 16) for s in range(pulses)]

        def own_rows(step, carry):
            at = pl.ds(pl.multiple_of(step * 16, 16), 16)
            at_im = pl.ds(pl.multiple_of(segment + step * 16, 16), 16)
            total_re = jnp.zeros((16, blocks), F32)
            total_im = jnp.zeros((16, blocks), F32)
            for s in range(pulses):
                real = comp_ref[s, at, :].astype(F32)
                imag = comp_ref[s, at_im, :].astype(F32)
                total_re = total_re + (own_re[s] * real - own_im[s] * imag)
                total_im = total_im + (own_im[s] * real + own_re[s] * imag)
            acc_ref[b, 0, at, :] = total_re
            acc_ref[b, 1, at, :] = total_im
            return carry

        lax.fori_loop(0, segment // 16, own_rows, 0)

    def section_terms(s):
        upper = (me >> s) & 1
        found = []
        for c in range(2):
            f = fraction_ref[s, c]
            o = offsets_ref[s, c]
            turn = lax.rem(17 * (o + 100), 20).astype(F32) * 0.05
            cosine, sine = cos_sin_cycles(turn + 0.85 * f)
            found.append(list(cubic_weights(f)) + [cosine * math.sqrt(0.5), sine * math.sqrt(0.5)])
        is_upper = jnp.zeros(fraction_ref.shape[2:], jnp.int32) + upper == 1
        own = [jnp.where(is_upper, u, l) for l, u in zip(*found)]
        far = [jnp.where(is_upper, l, u) for l, u in zip(*found)]
        return own, far

    terms = [section_terms(s) for s in range(SECTIONS)]

    def merge_copy(s, b):
        return pltpu.make_async_remote_copy(
            src_ref=image_ref.at[s, b],
            dst_ref=other_ref.at[s, b],
            send_sem=merge_send.at[s, b],
            recv_sem=merge_recv.at[s, b],
            device_id={"sub": me ^ (1 << s)},
            device_id_type=MESH,
        )

    lane = lax.broadcasted_iota(jnp.int32, (HALO, blocks), 1)

    def widen(source):
        for part in range(2):
            value = source[part].astype(F32)
            wide_ref[part, HALO : HALO + segment, :] = value
            wide_ref[part, 0:HALO, :] = jnp.where(
                lane > 0, pltpu.roll(value[segment - HALO :], 1, 1), 0.0
            )
            wide_ref[part, HALO + segment :, :] = jnp.where(
                lane < blocks - 1, pltpu.roll(value[:HALO], blocks - 1, 1), 0.0
            )

    def interpolate(s, b, far, store):
        upper = (me >> s) & 1
        child = 1 - upper if far else upper
        first = shift_ref[s, child, 0, b] + (HALO - 1)
        w0, w1, w2, w3, cosine, sine = [
            jnp.broadcast_to(t[:, b : b + 1], (CHUNK, blocks)) for t in terms[s][int(far)]
        ]

        def rows(step, carry):
            start = first + step * CHUNK
            sums = []
            for part in range(2):
                taps = [wide_ref[part, pl.ds(start + t, CHUNK), :] for t in range(4)]
                sums.append(w0 * taps[0] + w1 * taps[1] + w2 * taps[2] + w3 * taps[3])
            at = pl.ds(pl.multiple_of(step * CHUNK, CHUNK), CHUNK)
            store(at, 0, cosine * sums[0] - sine * sums[1])
            store(at, 1, sine * sums[0] + cosine * sums[1])
            return carry

        lax.fori_loop(0, segment // CHUNK, rows, 0)

    def own_side(s, b):
        widen(image_ref.at[s, b])

        def store(at, part, value):
            acc_ref[b, part, at, :] = value

        interpolate(s, b, False, store)

    def far_side(s, b):
        merge_copy(s, b).wait_recv()
        widen(other_ref.at[s, b])
        if s + 1 < SECTIONS:

            def store(at, part, value):
                image_ref[s + 1, b, part, at, :] = (acc_ref[b, part, at, :] + value).astype(BF16)

            interpolate(s, b, True, store)
            merge_copy(s + 1, b).start()
            own_side(s + 1, b)
        else:

            def store(at, part, value):
                acc_ref[b, part, at, :] = acc_ref[b, part, at, :] + value

            interpolate(s, b, True, store)
            for part in range(2):
                out_ref[part, b] = jnp.transpose(acc_ref[b, part]).astype(BF16)

    for q in range(moved):
        hand_copy(q).wait_recv()
        pair_copy(q, sector).start()
    for q in range(moved):
        pair_copy(q, 1 - sector).wait_recv()
        stack(hand_ref[q], pulses + q)
        if q % 2 == 1:
            compress(pulses + q - 1, 2)
        elif q == moved - 1:
            compress(pulses + q, 1)

    for b in range(beams):
        far_re = [spread(weight_re, b, q, 16) for q in range(moved)]
        far_im = [spread(weight_im, b, q, 16) for q in range(moved)]

        def first_rows(step, carry):
            at = pl.ds(pl.multiple_of(step * 16, 16), 16)
            at_im = pl.ds(pl.multiple_of(segment + step * 16, 16), 16)
            total_re = acc_ref[b, 0, at, :]
            total_im = acc_ref[b, 1, at, :]
            for q in range(moved):
                real = comp_ref[pulses + q, at, :].astype(F32)
                imag = comp_ref[pulses + q, at_im, :].astype(F32)
                total_re = total_re + (far_re[q] * real - far_im[q] * imag)
                total_im = total_im + (far_im[q] * real + far_re[q] * imag)
            image_ref[0, b, 0, at, :] = total_re.astype(BF16)
            image_ref[0, b, 1, at, :] = total_im.astype(BF16)
            return carry

        lax.fori_loop(0, segment // 16, first_rows, 0)
        merge_copy(0, b).start()
    for b in range(beams):
        own_side(0, b)
    order = sorted(
        [(2 * s + b, -s, s, b) for s in range(SECTIONS - 1) for b in range(beams)]
        + [(4 * SECTIONS + b, 0, SECTIONS - 1, b) for b in range(beams)]
    )
    for _, _, s, b in order:
        far_side(s, b)

    def end_count(step, carry):
        count_copy(step, me).wait_send()
        return carry

    lax.fori_loop(1, owners, end_count, 0)
    for q in range(moved):
        hand_copy(q).wait_send()
        pair_copy(q, sector).wait_send()
    for s in range(SECTIONS):
        for b in range(beams):
            merge_copy(s, b).wait_send()


def on_device(owners, ingest, replica, counts, track_list, deviation, offsets, fraction):
    slots, blocks, both = ingest.shape
    pulses = slots // 2
    segment = both // 2
    taps = replica.shape[1]
    depth = (segment + taps) // segment
    moved = pulses - 1
    vmem = pl.BlockSpec(memory_space=pltpu.VMEM)
    hbm = pl.BlockSpec(memory_space=pl.ANY)
    dma = pltpu.SemaphoreType.DMA
    result = pl.pallas_call(
        functools.partial(kernel, owners, pulses),
        out_shape=jax.ShapeDtypeStruct((2, pulses, blocks, segment), BF16),
        in_specs=[hbm] * 7,
        out_specs=vmem,
        scratch_shapes=[
            pltpu.VMEM(ingest.shape, BF16),
            pltpu.VMEM(replica.shape, BF16),
            pltpu.SMEM(counts.shape, jnp.int32),
            pltpu.VMEM((1, slots), jnp.int32),
            pltpu.VMEM((1, pulses), F32),
            pltpu.SMEM(offsets.shape, jnp.int32),
            pltpu.VMEM(offsets.shape, jnp.int32),
            pltpu.VMEM(fraction.shape, F32),
            dma((8,)),
            pltpu.VMEM((8, 128), jnp.int32),
            pltpu.VMEM((owners, 8, 128), jnp.int32),
            pltpu.VMEM((both, depth * both), BF16),
            pltpu.VMEM(((pulses + moved) * blocks, depth * both), BF16),
            pltpu.VMEM((pulses + moved, both, blocks), BF16),
            pltpu.VMEM((moved, blocks // 2, both), BF16),
            pltpu.VMEM((moved, blocks, both), BF16),
            pltpu.VMEM((pulses, blocks, both), BF16),
            pltpu.VMEM((pulses, 2, segment, blocks), F32),
            pltpu.VMEM((SECTIONS, pulses, 2, segment, blocks), BF16),
            pltpu.VMEM((SECTIONS, pulses, 2, segment, blocks), BF16),
            pltpu.VMEM((2, segment + 2 * HALO, blocks), F32),
            dma((owners,)),
            dma((owners,)),
            dma((moved,)),
            dma((moved,)),
            dma((moved,)),
            dma((moved,)),
            dma((SECTIONS, pulses)),
            dma((SECTIONS, pulses)),
        ],
        compiler_params=pltpu.CompilerParams(
            collective_id=0, has_side_effects=True, vmem_limit_bytes=40 * 1024 * 1024
        ),
    )(
        ingest,
        replica,
        counts,
        track_list.reshape(1, slots),
        deviation.reshape(1, pulses),
        offsets,
        fraction,
    )
    return result.reshape(2, 1, pulses, blocks * segment)


def solution(mesh):
    return jax.shard_map(
        functools.partial(on_device, mesh.shape["sub"]),
        mesh=mesh,
        in_specs=(
            P(("groups", "sub"), None, None),
            P(),
            P(("groups", "sub")),
            P(("groups", "sub")),
            P(("groups", "sub")),
            P(None, None, ("groups", "sub"), "sector"),
            P(None, None, ("groups", "sub"), "sector"),
        ),
        out_specs=P(None, ("groups", "sub"), "sector", None),
        check_vma=False,
    )
```

```python
import functools
import math

import jax
import jax.numpy as jnp
from jax import lax
from jax.experimental import pallas as pl
from jax.experimental.pallas import tpu as pltpu
from jax.sharding import PartitionSpec as P

SECTIONS = 3
HALO = 72
CHUNK = 32
MESH = pl.DeviceIdType.MESH
F32 = jnp.float32
BF16 = jnp.bfloat16


def cos_sin_cycles(cycles):
    angle = (2.0 * math.pi) * (cycles - jnp.floor(cycles + 0.5))
    return jnp.cos(angle), jnp.sin(angle)


def cubic_weights(fractions):
    square = fractions * fractions
    cubed = square * fractions
    return (
        -0.5 * cubed + square - 0.5 * fractions,
        1.5 * cubed - 2.5 * square + 1.0,
        -1.5 * cubed + 2.0 * square + 0.5 * fractions,
        0.5 * cubed - 0.5 * square,
    )


def build_filter(replica_ref, filter_ref, segment, parts):
    taps = replica_ref.shape[1]
    window = segment + taps
    row = lax.broadcasted_iota(jnp.int32, (16, window), 0)
    for part in parts:
        response = replica_ref[part : part + 1, :].astype(F32)
        line = jnp.concatenate([response, jnp.zeros((1, segment), F32)], axis=1)
        base = jnp.broadcast_to(line, (16, window))
        for bit in range(4):
            base = jnp.where((row >> bit) & 1 == 1, pltpu.roll(base, 1 << bit, 1), base)
        for group in range(segment // 16):
            band = base if group == 0 else pltpu.roll(base, 16 * group, 1)
            band_up = band.astype(BF16)
            band_neg = (-band).astype(BF16)
            rows = slice(16 * group, 16 * group + 16)
            rows_low = slice(segment + 16 * group, segment + 16 * group + 16)
            for j in range(window // segment):
                piece = slice(j * segment, (j + 1) * segment)
                re_at = slice(2 * j * segment, (2 * j + 1) * segment)
                im_at = slice((2 * j + 1) * segment, (2 * j + 2) * segment)
                if part == 0:
                    filter_ref[rows, re_at] = band_up[:, piece]
                    filter_ref[rows_low, im_at] = band_up[:, piece]
                else:
                    filter_ref[rows, im_at] = band_up[:, piece]
                    filter_ref[rows_low, re_at] = band_neg[:, piece]


def kernel(
    owners,
    pulses,
    ingest_hbm,
    replica_hbm,
    counts_hbm,
    track_hbm,
    deviation_hbm,
    offsets_hbm,
    fraction_hbm,
    out_ref,
    ingest_ref,
    replica_ref,
    counts_ref,
    track_ref,
    deviation_ref,
    shift_ref,
    offsets_ref,
    fraction_ref,
    load_sem,
    count_mine,
    count_all,
    filter_ref,
    stacked_ref,
    comp_ref,
    excess_ref,
    hand_ref,
    acc_ref,
    image_ref,
    other_ref,
    wide_ref,
    count_send,
    count_recv,
    hand_send,
    hand_recv,
    pair_send,
    pair_recv,
    merge_send,
    merge_recv,
):
    slots, blocks, both = ingest_ref.shape
    segment = both // 2
    moved = pulses - 1
    me = lax.axis_index("sub")
    sector = lax.axis_index("sector")

    def peer(step):
        return lax.rem(me + step, owners)

    barrier = pltpu.get_barrier_semaphore()

    def greet(step, carry):
        pl.semaphore_signal(barrier, inc=1, device_id={"sub": peer(step)}, device_id_type=MESH)
        return carry

    lax.fori_loop(1, owners, greet, 0)
    pl.semaphore_signal(barrier, inc=1, device_id={"sector": 1 - sector}, device_id_type=MESH)
    loads = [
        pltpu.make_async_copy(source, target, load_sem.at[i])
        for i, (source, target) in enumerate(
            [
                (replica_hbm, replica_ref),
                (counts_hbm, counts_ref),
                (track_hbm, track_ref),
                (deviation_hbm, deviation_ref),
                (offsets_hbm, shift_ref),
                (offsets_hbm, offsets_ref),
                (fraction_hbm, fraction_ref),
                (ingest_hbm, ingest_ref),
            ]
        )
    ]
    for load in loads:
        load.start()
    loads[0].wait()
    build_filter(replica_ref, filter_ref, segment, [0, 1])
    loads[7].wait()

    def stack(data, first):
        rows = slice(first * blocks, (first + 1) * blocks)
        stacked_ref[rows, 0:both] = data
        wide = data.astype(F32)
        at = lax.broadcasted_iota(jnp.int32, wide.shape, 0)
        for j in range(1, stacked_ref.shape[1] // both):
            later = jnp.where(at < blocks - j, pltpu.roll(wide, blocks - j, 0), 0.0)
            stacked_ref[rows, j * both : (j + 1) * both] = later.astype(BF16)

    def compress(first, many):
        found = lax.dot_general(
            filter_ref[...],
            stacked_ref[first * blocks : (first + many) * blocks, :],
            (((1,), (1,)), ((), ())),
            preferred_element_type=F32,
        ).astype(BF16)
        for i in range(many):
            comp_ref[first + i] = found[:, i * blocks : (i + 1) * blocks]

    def compress_slots(first, many):
        for slot in range(first, first + many):
            stack(ingest_ref[slot], slot)
        for slot in range(first, first + many, 2):
            compress(slot, 2)

    early = slots // 4 * 2
    compress_slots(0, early)
    loads[1].wait()
    count_mine[...] = jnp.zeros(count_mine.shape, jnp.int32) + counts_ref[0]
    pl.semaphore_wait(barrier, owners)

    def count_copy(step, source):
        return pltpu.make_async_remote_copy(
            src_ref=count_mine,
            dst_ref=count_all.at[source],
            send_sem=count_send.at[step],
            recv_sem=count_recv.at[source],
            device_id={"sub": peer(step)},
            device_id_type=MESH,
        )

    def send_count(step, carry):
        count_copy(step, me).start()
        return carry

    lax.fori_loop(1, owners, send_count, 0)

    compress_slots(early, slots - early)
    for load in loads[2:7]:
        load.wait()

    def wait_count(step, carry):
        count_copy(step, peer(step)).wait_recv()
        return carry

    lax.fori_loop(1, owners, wait_count, 0)
    count_all[me] = count_mine[...]

    def add_count(source, total):
        return total + jnp.where(source < me, count_all[source], 0)

    starts = lax.fori_loop(0, owners, add_count, jnp.zeros((8, 128), jnp.int32))
    track = track_ref[...]
    place = starts[0:1, 0:1] - me * pulses + track

    def chosen(target):
        return jnp.where((place == target) & (track >= 0), 1.0, 0.0).astype(F32)

    def pick_at(target):
        pick = chosen(target)
        return [
            jnp.broadcast_to(pick[:, s : s + 1], (16, blocks)).astype(BF16) for s in range(slots)
        ]

    excess_picks = [pick_at(pulses + q) for q in range(moved)]

    def pick_rows(step, carry):
        at = pl.ds(pl.multiple_of(sector * segment + step * 16, 16), 16)
        to = pl.ds(pl.multiple_of(step * 16, 16), 16)
        values = [comp_ref[s, at, :] for s in range(slots)]
        for q, pick in enumerate(excess_picks):
            total = pick[0] * values[0]
            for s in range(1, slots):
                total = total + pick[s] * values[s]
            excess_ref[q, to, :] = total
        return carry

    lax.fori_loop(0, segment // 16, pick_rows, 0)

    def hand_copy(q):
        return pltpu.make_async_remote_copy(
            src_ref=excess_ref.at[q],
            dst_ref=hand_ref.at[q, sector],
            send_sem=hand_send.at[q],
            recv_sem=hand_recv.at[q],
            device_id={"sub": peer(1)},
            device_id_type=MESH,
        )

    def pair_copy(q, part):
        return pltpu.make_async_remote_copy(
            src_ref=hand_ref.at[q, part],
            dst_ref=hand_ref.at[q, part],
            send_sem=pair_send.at[q],
            recv_sem=pair_recv.at[q],
            device_id={"sector": 1 - sector},
            device_id_type=MESH,
        )

    @pl.when(me < owners - 1)
    def _():
        for q in range(moved):
            hand_copy(q).start()

    @pl.when(me == 0)
    def _():
        hand_ref[...] = jnp.zeros(hand_ref.shape, BF16)

    beams = pulses
    beam_index = lax.broadcasted_iota(jnp.int32, (beams, 1), 0) + sector * beams
    beam_angle = (beam_index.astype(F32) + 0.5) / (2.0 * beams) - 0.5
    pulse_index = lax.broadcasted_iota(jnp.int32, (1, pulses), 1).astype(F32)
    position = 2.0 * (pulse_index - (pulses - 1) / 2.0) + deviation_ref[...]
    cosine, sine = cos_sin_cycles(position * beam_angle)
    scale = 1.0 / math.sqrt(pulses)
    weight_re = (cosine * scale).astype(BF16).astype(F32)
    weight_im = (sine * scale).astype(BF16).astype(F32)
    slot_re = jnp.zeros((beams, slots), F32)
    slot_im = jnp.zeros((beams, slots), F32)
    for p in range(pulses):
        select = chosen(p)
        slot_re = slot_re + weight_re[:, p : p + 1] * select
        slot_im = slot_im + weight_im[:, p : p + 1] * select

    def spread(values, b, s, rows):
        return jnp.broadcast_to(values[b : b + 1, s : s + 1], (rows, blocks))

    for b in range(beams):
        own_re = [spread(slot_re, b, s, 16) for s in range(slots)]
        own_im = [spread(slot_im, b, s, 16) for s in range(slots)]

        def own_rows(step, carry):
            at = pl.ds(pl.multiple_of(step * 16, 16), 16)
            at_im = pl.ds(pl.multiple_of(segment + step * 16, 16), 16)
            total_re = jnp.zeros((16, blocks), F32)
            total_im = jnp.zeros((16, blocks), F32)
            for s in range(slots):
                real = comp_ref[s, at, :].astype(F32)
                imag = comp_ref[s, at_im, :].astype(F32)
                total_re = total_re + (own_re[s] * real - own_im[s] * imag)
                total_im = total_im + (own_im[s] * real + own_re[s] * imag)
            acc_ref[b, 0, at, :] = total_re
            acc_ref[b, 1, at, :] = total_im
            return carry

        lax.fori_loop(0, segment // 16, own_rows, 0)

    def section_terms(s):
        upper = (me >> s) & 1
        found = []
        for c in range(2):
            f = fraction_ref[s, c]
            o = offsets_ref[s, c]
            turn = lax.rem(17 * (o + 100), 20).astype(F32) * 0.05
            cosine, sine = cos_sin_cycles(turn + 0.85 * f)
            found.append(list(cubic_weights(f)) + [cosine * math.sqrt(0.5), sine * math.sqrt(0.5)])
        is_upper = jnp.zeros(fraction_ref.shape[2:], jnp.int32) + upper == 1
        own = [jnp.where(is_upper, u, l) for l, u in zip(*found)]
        far = [jnp.where(is_upper, l, u) for l, u in zip(*found)]
        return own, far

    terms = [section_terms(s) for s in range(SECTIONS)]

    def merge_copy(s, b):
        return pltpu.make_async_remote_copy(
            src_ref=image_ref.at[s, b],
            dst_ref=other_ref.at[s, b],
            send_sem=merge_send.at[s, b],
            recv_sem=merge_recv.at[s, b],
            device_id={"sub": me ^ (1 << s)},
            device_id_type=MESH,
        )

    lane = lax.broadcasted_iota(jnp.int32, (HALO, blocks), 1)

    def widen(source):
        for part in range(2):
            value = source[part].astype(F32)
            wide_ref[part, HALO : HALO + segment, :] = value
            wide_ref[part, 0:HALO, :] = jnp.where(
                lane > 0, pltpu.roll(value[segment - HALO :], 1, 1), 0.0
            )
            wide_ref[part, HALO + segment :, :] = jnp.where(
                lane < blocks - 1, pltpu.roll(value[:HALO], blocks - 1, 1), 0.0
            )

    def interpolate(s, b, far, store):
        upper = (me >> s) & 1
        child = 1 - upper if far else upper
        first = shift_ref[s, child, 0, b] + (HALO - 1)
        w0, w1, w2, w3, cosine, sine = [
            jnp.broadcast_to(t[:, b : b + 1], (CHUNK, blocks)) for t in terms[s][int(far)]
        ]

        def rows(step, carry):
            start = first + step * CHUNK
            sums = []
            for part in range(2):
                taps = [wide_ref[part, pl.ds(start + t, CHUNK), :] for t in range(4)]
                sums.append(w0 * taps[0] + w1 * taps[1] + w2 * taps[2] + w3 * taps[3])
            at = pl.ds(pl.multiple_of(step * CHUNK, CHUNK), CHUNK)
            store(at, 0, cosine * sums[0] - sine * sums[1])
            store(at, 1, sine * sums[0] + cosine * sums[1])
            return carry

        lax.fori_loop(0, segment // CHUNK, rows, 0)

    def own_side(s, b):
        widen(image_ref.at[s, b])

        def store(at, part, value):
            acc_ref[b, part, at, :] = value

        interpolate(s, b, False, store)

    def far_side(s, b):
        if s == 0 and b + 1 < beams:
            merge_copy(0, b).wait_send()
            merge_copy(0, b + 1).start()
        merge_copy(s, b).wait_recv()
        widen(other_ref.at[s, b])
        if s + 1 < SECTIONS:

            def store(at, part, value):
                image_ref[s + 1, b, part, at, :] = (acc_ref[b, part, at, :] + value).astype(BF16)

            interpolate(s, b, True, store)
            merge_copy(s + 1, b).start()
            own_side(s + 1, b)
        else:

            def store(at, part, value):
                acc_ref[b, part, at, :] = acc_ref[b, part, at, :] + value

            interpolate(s, b, True, store)
            for part in range(2):
                out_ref[part, b] = jnp.transpose(acc_ref[b, part]).astype(BF16)

    @pl.when(me > 0)
    def _():
        for q in range(moved):
            hand_copy(q).wait_recv()
            pair_copy(q, sector).start()
        for q in range(moved):
            pair_copy(q, 1 - sector).wait_recv()

    for b in range(beams):
        far_re = [spread(weight_re, b, q, 16) for q in range(moved)]
        far_im = [spread(weight_im, b, q, 16) for q in range(moved)]

        def first_rows(step, carry):
            at = pl.ds(pl.multiple_of(step * 16, 16), 16)
            total_re = acc_ref[b, 0, at, :]
            total_im = acc_ref[b, 1, at, :]
            for q in range(moved):
                real = hand_ref[q, 0, at, :].astype(F32)
                imag = hand_ref[q, 1, at, :].astype(F32)
                total_re = total_re + (far_re[q] * real - far_im[q] * imag)
                total_im = total_im + (far_im[q] * real + far_re[q] * imag)
            image_ref[0, b, 0, at, :] = total_re.astype(BF16)
            image_ref[0, b, 1, at, :] = total_im.astype(BF16)
            return carry

        lax.fori_loop(0, segment // 16, first_rows, 0)
        if b == 0:
            merge_copy(0, b).start()
    for b in range(beams):
        own_side(0, b)
    order = sorted(
        [(2 * s + b, -s, s, b) for s in range(SECTIONS - 1) for b in range(beams)]
        + [(4 * SECTIONS + b, 0, SECTIONS - 1, b) for b in range(beams)]
    )
    for _, _, s, b in order:
        far_side(s, b)

    def end_count(step, carry):
        count_copy(step, me).wait_send()
        return carry

    lax.fori_loop(1, owners, end_count, 0)

    @pl.when(me < owners - 1)
    def _():
        for q in range(moved):
            hand_copy(q).wait_send()

    @pl.when(me > 0)
    def _():
        for q in range(moved):
            pair_copy(q, sector).wait_send()

    for s in range(SECTIONS):
        for b in range(beams):
            if s > 0 or b == beams - 1:
                merge_copy(s, b).wait_send()


def on_device(owners, ingest, replica, counts, track_list, deviation, offsets, fraction):
    slots, blocks, both = ingest.shape
    pulses = slots // 2
    segment = both // 2
    taps = replica.shape[1]
    depth = (segment + taps) // segment
    moved = pulses - 1
    vmem = pl.BlockSpec(memory_space=pltpu.VMEM)
    hbm = pl.BlockSpec(memory_space=pl.ANY)
    dma = pltpu.SemaphoreType.DMA
    result = pl.pallas_call(
        functools.partial(kernel, owners, pulses),
        out_shape=jax.ShapeDtypeStruct((2, pulses, blocks, segment), BF16),
        in_specs=[hbm] * 7,
        out_specs=vmem,
        scratch_shapes=[
            pltpu.VMEM(ingest.shape, BF16),
            pltpu.VMEM(replica.shape, BF16),
            pltpu.SMEM(counts.shape, jnp.int32),
            pltpu.VMEM((1, slots), jnp.int32),
            pltpu.VMEM((1, pulses), F32),
            pltpu.SMEM(offsets.shape, jnp.int32),
            pltpu.VMEM(offsets.shape, jnp.int32),
            pltpu.VMEM(fraction.shape, F32),
            dma((8,)),
            pltpu.VMEM((8, 128), jnp.int32),
            pltpu.VMEM((owners, 8, 128), jnp.int32),
            pltpu.VMEM((both, depth * both), BF16),
            pltpu.VMEM((slots * blocks, depth * both), BF16),
            pltpu.VMEM((slots, both, blocks), BF16),
            pltpu.VMEM((moved, segment, blocks), BF16),
            pltpu.VMEM((moved, 2, segment, blocks), BF16),
            pltpu.VMEM((pulses, 2, segment, blocks), F32),
            pltpu.VMEM((SECTIONS, pulses, 2, segment, blocks), BF16),
            pltpu.VMEM((SECTIONS, pulses, 2, segment, blocks), BF16),
            pltpu.VMEM((2, segment + 2 * HALO, blocks), F32),
            dma((owners,)),
            dma((owners,)),
            dma((moved,)),
            dma((moved,)),
            dma((moved,)),
            dma((moved,)),
            dma((SECTIONS, pulses)),
            dma((SECTIONS, pulses)),
        ],
        compiler_params=pltpu.CompilerParams(
            collective_id=0, has_side_effects=True, vmem_limit_bytes=60 * 1024 * 1024
        ),
    )(
        ingest,
        replica,
        counts,
        track_list.reshape(1, slots),
        deviation.reshape(1, pulses),
        offsets,
        fraction,
    )
    return result.reshape(2, 1, pulses, blocks * segment)


def solution(mesh):
    return jax.shard_map(
        functools.partial(on_device, mesh.shape["sub"]),
        mesh=mesh,
        in_specs=(
            P(("groups", "sub"), None, None),
            P(),
            P(("groups", "sub")),
            P(("groups", "sub")),
            P(("groups", "sub")),
            P(None, None, ("groups", "sub"), "sector"),
            P(None, None, ("groups", "sub"), "sector"),
        ),
        out_specs=P(None, ("groups", "sub"), "sector", None),
        check_vma=False,
    )
```
